32 devices in a mesh: dp: 2 (over x), expert: 16 (over z, y, core).
Axes of the slice: x: 2, y: 2, z: 4, core: 2. Of those that a mesh axis runs over, the one named last changes fastest.
Arguments:
- tokens: bfloat16 [4096, 4096], P('expert', 'dp'), may hold values from -6 to 6
- out_grad: bfloat16 [4096, 4096], P('expert', 'dp'), may hold values from -3 to 3
- expert_ids: int32 [4096, 2], P('expert'), may hold values from 0 to 15, as said below
- gate_probs: float32 [4096, 2], P('expert'), may hold values from 0.25 to 1
- w_gate: bfloat16 [16, 4096, 1024], P('expert', 'dp'), may hold values from -0.09375 to 0.09375
- w_up: bfloat16 [16, 4096, 1024], P('expert', 'dp'), may hold values from -0.09375 to 0.09375
- w_down: bfloat16 [16, 1024, 4096], P('expert', None, 'dp'), may hold values from -0.1875 to 0.1875
Outputs:
- token_grad: bfloat16 [4096, 4096], P('expert', 'dp')
- grad_w_gate: float32 [16, 4096, 1024], P('expert', 'dp')
- grad_w_up: float32 [16, 4096, 1024], P('expert', 'dp')
- grad_w_down: float32 [16, 1024, 4096], P('expert', None, 'dp')
The draws below stay inside these ranges and needn't reach their ends.
Inputs may be any that keep to these rules, and one draw needn't show every extreme that they name: `expert_ids`: A token's two ids differ. Among the tokens of one aligned block of 256 tokens no expert is named more than 32 times; 4 experts, the same for every block, are named exactly 32 times in each block.
All inputs are finite; a program needn't handle non-finite values.
Results may differ from the reference program's by a relative error of at most 0.02.
Values may be sent and summed in bfloat16 or wider, within the bound.
A program may use at most 128 MiB of HBM per device.

```python
import jax
import jax.numpy as jnp
from jax import lax

D = 4096
FF = 1024
TOK_DEV = 256
HOT = 4
MOST = 32
EXPERTS = 16
TOKENS = 4096
N_DP = 2
N_EXPERT = 16


def draw_expert_ids(key, part):
    blocks = TOKENS // TOK_DEV
    pick_count = 2 * TOK_DEV
    total_slots = EXPERTS * MOST
    expert_order = jax.random.permutation(jax.random.fold_in(key, 11), EXPERTS)
    expert_place = jnp.argsort(expert_order)
    is_hot = expert_place < HOT
    slot_expert = jnp.repeat(jnp.arange(EXPERTS, dtype=jnp.int32), MOST)
    slot_hot = is_hot[slot_expert]

    def one_block(block_key):
        shuffle = jax.random.permutation(jax.random.fold_in(block_key, 1), total_slots).astype(jnp.int32)
        slot_score = jnp.where(slot_hot, -1 - jnp.arange(total_slots, dtype=jnp.int32), shuffle)
        chosen = jnp.argsort(slot_score)[:pick_count]
        named_sorted = jnp.sort(slot_expert[chosen])
        paired = jnp.stack([named_sorted[:TOK_DEV], named_sorted[TOK_DEV:]], axis=1)
        paired = paired[jax.random.permutation(jax.random.fold_in(block_key, 2), TOK_DEV)]
        flip_pair = jax.random.randint(jax.random.fold_in(block_key, 3), (TOK_DEV, 1), 0, 2)
        return jnp.where(flip_pair == 1, paired[:, ::-1], paired)
    block_keys = jax.random.split(jax.random.fold_in(key, 12), blocks)
    return jax.vmap(one_block)(block_keys).reshape(TOKENS, 2).astype(jnp.int32)


def block_levels(key, shape, cuts, low, largest):
    def one(position, parts):
        draws = jax.random.uniform(jax.random.fold_in(jax.random.fold_in(key, 6), position), (parts,), jnp.float32, low / len(cuts), largest / len(cuts))
        return jnp.repeat(jnp.exp(draws), shape[position] // parts).reshape((-1,) + (1,) * (len(shape) - position - 1))

    gain = one(*cuts[0])
    for cut in cuts[1:]:
        gain = gain * one(*cut)
    return gain


def centred(key, extent, scale, most, shards=(), held_as=jnp.bfloat16):
    result = scale * jax.random.normal(key, extent, jnp.float32)
    if shards:
        result = result * block_levels(key, extent, shards, -0.22, 0.18)
    return jnp.clip(result, -most, most).astype(held_as)


def setup_inputs(seed: int = 0) -> dict:
    splits = jax.random.split(jax.random.key(seed), 8)
    return {
        "tokens": centred(splits[0], (TOKENS, D), 1.0, 6.0, ((0, 16), (1, 2))),
        "out_grad": centred(splits[1], (TOKENS, D), 0.5, 3.0, ((0, 16), (1, 2))),
        "expert_ids": draw_expert_ids(jax.random.fold_in(splits[7], 71), 0),
        "gate_probs": jnp.clip(0.25 + 0.75 * jax.random.uniform(splits[3], (TOKENS, 2), jnp.float32) ** block_levels(splits[3], (TOKENS, 2), ((0, 16),), -0.2, 0.2), 0.25, 1.0),
        "w_gate": centred(splits[4], (EXPERTS, D, FF), D ** -0.5, 0.09375, ((0, 16), (1, 2))),
        "w_up": centred(splits[5], (EXPERTS, D, FF), D ** -0.5, 0.09375, ((0, 16), (1, 2))),
        "w_down": centred(splits[6], (EXPERTS, FF, D), FF ** -0.5, 0.1875, ((0, 16), (2, 2))),
    }


def silu_parts(pre_gate):
    sigmoid_gate = jax.nn.sigmoid(pre_gate)
    return pre_gate * sigmoid_gate, sigmoid_gate * (1.0 + pre_gate * (1.0 - sigmoid_gate))


def rounded(values):
    return lax.optimization_barrier(values.astype(jnp.bfloat16)).astype(jnp.float32)


def reference(tokens, out_grad, expert_ids, gate_probs, w_gate, w_up, w_down):
    model_width = tokens.shape[1]
    slab_width = model_width // N_DP
    hidden_width = w_gate.shape[2]
    flat_ids = expert_ids.reshape(-1)
    owner_row = jnp.arange(flat_ids.shape[0], dtype=jnp.int32) // 2
    flat_probs = gate_probs.reshape(-1)
    capacity = N_EXPERT * MOST

    def per_expert(grad_total, expert):
        matches = flat_ids == expert
        chosen = jnp.nonzero(matches, size=capacity, fill_value=0)[0].astype(jnp.int32)
        live_rows = (jnp.arange(capacity, dtype=jnp.int32) < jnp.sum(matches.astype(jnp.int32)))[:, None]
        token_rows = owner_row[chosen]
        gathered = jnp.where(live_rows, tokens[token_rows], jnp.zeros((), tokens.dtype))
        scaled = jnp.where(live_rows, flat_probs[chosen][:, None] * out_grad[token_rows].astype(jnp.float32), 0.0).astype(jnp.bfloat16)
        gate_mat = w_gate[expert]
        up_mat = w_up[expert]
        down_mat = w_down[expert]
        pre_gate = jnp.zeros((capacity, hidden_width), jnp.float32)
        pre_up = jnp.zeros((capacity, hidden_width), jnp.float32)
        grad_act = jnp.zeros((capacity, hidden_width), jnp.float32)
        for block_index in range(N_DP):
            first_col = block_index * slab_width
            last_col = first_col + slab_width
            pre_gate = pre_gate + rounded(jnp.dot(gathered[:, first_col:last_col], gate_mat[first_col:last_col], preferred_element_type=jnp.float32))
            pre_up = pre_up + rounded(jnp.dot(gathered[:, first_col:last_col], up_mat[first_col:last_col], preferred_element_type=jnp.float32))
            grad_act = grad_act + rounded(jnp.dot(scaled[:, first_col:last_col], down_mat[:, first_col:last_col].T, preferred_element_type=jnp.float32))
        active, slope_gate = silu_parts(pre_gate)
        hidden = (active * pre_up).astype(jnp.bfloat16)
        grad_gate = (grad_act * pre_up * slope_gate).astype(jnp.bfloat16)
        grad_up = (grad_act * active).astype(jnp.bfloat16)
        pick_grad = jnp.dot(grad_gate, gate_mat.T, preferred_element_type=jnp.float32) + jnp.dot(grad_up, up_mat.T, preferred_element_type=jnp.float32)
        grad_total = grad_total.at[token_rows].add(jnp.where(live_rows, pick_grad, 0.0))
        gate_grads = jnp.dot(gathered.T, grad_gate, preferred_element_type=jnp.float32)
        up_grads = jnp.dot(gathered.T, grad_up, preferred_element_type=jnp.float32)
        down_grads = jnp.dot(hidden.T, scaled, preferred_element_type=jnp.float32)
        return grad_total, (gate_grads, up_grads, down_grads)

    initial = jnp.zeros(tokens.shape, jnp.float32)
    grad_total, stacked = lax.scan(per_expert, initial, jnp.arange(EXPERTS, dtype=jnp.int32))
    return grad_total.astype(jnp.bfloat16), stacked[0], stacked[1], stacked[2]
```

```python
import functools

import jax
import jax.numpy as jnp
from jax import lax
from jax.experimental import pallas as pl
from jax.experimental.pallas import tpu as pltpu
from jax.sharding import PartitionSpec as P

MOST = 32


contract_rows = (((0,), (0,)), ((), ()))
contract_cols = (((1,), (1,)), ((), ()))


def silu_parts(pre_gate):
    sigmoid_gate = jax.nn.sigmoid(pre_gate)
    return (pre_gate * sigmoid_gate, sigmoid_gate * (1.0 + pre_gate * (1.0 - sigmoid_gate)))


def local_grads(pre_gate, pre_up, grad_act):
    active, slope_gate = silu_parts(pre_gate)
    hidden = (active * pre_up).astype(jnp.bfloat16)
    grad_gate = (grad_act * pre_up * slope_gate).astype(jnp.bfloat16)
    grad_up = (grad_act * active).astype(jnp.bfloat16)
    return (hidden, grad_gate, grad_up)


def shards(tokens, out_grad, expert_ids, gate_probs, w_gate, w_up, w_down):
    tok_rows, slab_width = tokens.shape
    owners = lax.axis_size("expert")
    experts = owners * w_gate.shape[0]
    pick_ids = expert_ids.T.reshape(-1)
    onehot = (pick_ids[:, None] == jnp.arange(experts, dtype=jnp.int32)[None, :]).astype(jnp.int32)
    rank_in = jnp.sum((jnp.cumsum(onehot, axis=0) - 1) * onehot, axis=1)
    slot_of = pick_ids * MOST + rank_in
    placing = (jnp.arange(experts * MOST, dtype=jnp.int32)[:, None] == slot_of[None, :]).astype(
        jnp.bfloat16
    )
    row_pick = jnp.concatenate([tokens, tokens], axis=0)
    grad_pick = jnp.concatenate([out_grad, out_grad], axis=0)
    scaled = (gate_probs.T.reshape(-1)[:, None] * grad_pick.astype(jnp.float32)).astype(
        jnp.bfloat16
    )
    send_tokens = (
        jnp.dot(placing, row_pick, preferred_element_type=jnp.float32)
        .astype(jnp.bfloat16)
        .reshape(experts, MOST, slab_width)
    )
    send_grads = (
        jnp.dot(placing, scaled, preferred_element_type=jnp.float32)
        .astype(jnp.bfloat16)
        .reshape(experts, MOST, slab_width)
    )
    arrived_tokens, arrived_grads = (
        lax.all_to_all(send_tokens, "expert", split_axis=0, concat_axis=0, tiled=True),
        lax.all_to_all(send_grads, "expert", split_axis=0, concat_axis=0, tiled=True),
    )
    flat_tokens = arrived_tokens.reshape(-1, slab_width)
    flat_grads = arrived_grads.reshape(-1, slab_width)
    gate_mat = w_gate[0]
    up_mat = w_up[0]
    down_mat = w_down[0]
    part_gate = jnp.dot(flat_tokens, gate_mat, preferred_element_type=jnp.float32)
    part_up = jnp.dot(flat_tokens, up_mat, preferred_element_type=jnp.float32)
    part_act = lax.dot_general(
        flat_grads, down_mat, contract_cols, preferred_element_type=jnp.float32
    )
    pre_gate, pre_up, grad_act = (
        lax.psum(part_gate.astype(jnp.bfloat16), "dp").astype(jnp.float32),
        lax.psum(part_up.astype(jnp.bfloat16), "dp").astype(jnp.float32),
        lax.psum(part_act.astype(jnp.bfloat16), "dp").astype(jnp.float32),
    )
    hidden, grad_gate, grad_up = local_grads(pre_gate, pre_up, grad_act)
    slot_grad = lax.dot_general(
        grad_gate, gate_mat, contract_cols, preferred_element_type=jnp.float32
    )
    slot_grad = slot_grad + lax.dot_general(
        grad_up, up_mat, contract_cols, preferred_element_type=jnp.float32
    )
    gate_grads = lax.dot_general(
        flat_tokens, grad_gate, contract_rows, preferred_element_type=jnp.float32
    )[None]
    up_grads = lax.dot_general(
        flat_tokens, grad_up, contract_rows, preferred_element_type=jnp.float32
    )[None]
    down_grads = lax.dot_general(
        hidden, flat_grads, contract_rows, preferred_element_type=jnp.float32
    )[None]
    returned = lax.all_to_all(
        slot_grad.reshape(experts, MOST, slab_width).astype(jnp.bfloat16),
        "expert",
        split_axis=0,
        concat_axis=0,
        tiled=True,
    ).astype(jnp.float32)
    flat_back = returned.reshape(experts * MOST, slab_width)
    per_pick = jnp.take(flat_back, slot_of, axis=0)
    token_grad = (per_pick[:tok_rows] + per_pick[tok_rows:]).astype(jnp.bfloat16)
    return (token_grad, gate_grads, up_grads, down_grads)


GROUP = 4
TILE = 256


def partner_of(me, k, owners):
    result = 0
    bit = 1
    while bit < owners:
        digit = (me // bit) % 2
        result = result + bit * ((1 - digit) if k & bit else digit)
        bit *= 2
    return result


def exchange_kernel(
    owners,
    send_tokens,
    send_grads,
    w_gate,
    w_up,
    w_down,
    got_tokens,
    got_grads,
    hidden,
    grad_gate,
    grad_up,
    returned,
    gate_mat,
    up_mat,
    down_mat,
    part_pre,
    part_act,
    peer_pre,
    peer_act,
    slot_grad,
    load_sem,
    own_sem,
    tok_send,
    tok_recv,
    grad_send,
    grad_recv,
    pre_send,
    pre_recv,
    act_send,
    act_recv,
    back_send,
    back_recv,
):
    me = lax.axis_index("expert")
    other = 1 - lax.axis_index("dp")
    depth, width = w_gate.shape
    mesh_ids = pl.DeviceIdType.MESH

    loads = [
        pltpu.make_async_copy(source, target, load_sem.at[i])
        for i, (source, target) in enumerate(
            ((w_gate, gate_mat), (w_up, up_mat), (w_down, down_mat))
        )
    ]
    for load in loads:
        load.start()
    own = [
        pltpu.make_async_copy(source.at[pl.ds(0, MOST)], target.at[pl.ds(0, MOST)], own_sem.at[i])
        for i, (source, target) in enumerate(((send_tokens, got_tokens), (send_grads, got_grads)))
    ]
    for copy in own:
        copy.start()

    barrier = pltpu.get_barrier_semaphore()
    for k in range(1, owners):
        pl.semaphore_signal(
            barrier, inc=1, device_id={"expert": partner_of(me, k, owners)}, device_id_type=mesh_ids
        )
    pl.semaphore_signal(barrier, inc=1, device_id={"dp": other}, device_id_type=mesh_ids)
    pl.semaphore_wait(barrier, owners)

    def to_partner(k, source, target, send_sem, recv_sem):
        rows = pl.ds(k * MOST, MOST)
        return pltpu.make_async_remote_copy(
            src_ref=source.at[rows],
            dst_ref=target.at[rows],
            send_sem=send_sem.at[k],
            recv_sem=recv_sem.at[k],
            device_id={"expert": partner_of(me, k, owners)},
            device_id_type=mesh_ids,
        )

    def to_other(g, source, target, send_sem, recv_sem):
        rows = pl.ds(g * GROUP * MOST, GROUP * MOST)
        return pltpu.make_async_remote_copy(
            src_ref=source.at[rows],
            dst_ref=target.at[rows],
            send_sem=send_sem.at[g],
            recv_sem=recv_sem.at[g],
            device_id={"dp": other},
            device_id_type=mesh_ids,
        )

    groups = owners // GROUP
    tok_copies = {
        k: to_partner(k, send_tokens, got_tokens, tok_send, tok_recv) for k in range(1, owners)
    }
    grad_copies = {
        k: to_partner(k, send_grads, got_grads, grad_send, grad_recv) for k in range(1, owners)
    }
    pre_copies = [to_other(g, part_pre, peer_pre, pre_send, pre_recv) for g in range(groups)]
    act_copies = [to_other(g, part_act, peer_act, act_send, act_recv) for g in range(groups)]
    back_copies = {
        k: to_partner(k, slot_grad, returned, back_send, back_recv) for k in range(1, owners)
    }

    half = owners // 2
    near = list(range(1, half))
    far = list(range(half, owners))
    for copies in (tok_copies, grad_copies):
        for i in range(GROUP):
            copies[far[i]].start()
            for k in near[2 * i : 2 * i + 2]:
                copies[k].start()
    for first in range(GROUP, half, GROUP):
        for copies in (tok_copies, grad_copies):
            for k in far[first : first + GROUP]:
                copies[k].start()

    def members(g):
        return range(g * GROUP, (g + 1) * GROUP)

    def arrive(g, copies, own_copy):
        for k in members(g):
            if k == 0:
                own_copy.wait()
            else:
                copies[k].wait_recv()

    def pre_stage(g):
        arrive(g, tok_copies, own[0])
        rows = pl.ds(g * GROUP * MOST, GROUP * MOST)

        @pl.loop(0, width // TILE)
        def _(c):
            cols = pl.ds(pl.multiple_of(c * TILE, TILE), TILE)
            up_cols = pl.ds(pl.multiple_of(width + c * TILE, TILE), TILE)
            block = got_tokens[rows, :]
            part_pre[rows, cols] = jnp.dot(
                block, gate_mat[:, cols], preferred_element_type=jnp.float32
            ).astype(jnp.bfloat16)
            part_pre[rows, up_cols] = jnp.dot(
                block, up_mat[:, cols], preferred_element_type=jnp.float32
            ).astype(jnp.bfloat16)

        pre_copies[g].start()

    def act_stage(g):
        arrive(g, grad_copies, own[1])
        rows = pl.ds(g * GROUP * MOST, GROUP * MOST)

        @pl.loop(0, width // TILE)
        def _(c):
            cols = pl.ds(pl.multiple_of(c * TILE, TILE), TILE)
            part_act[rows, cols] = lax.dot_general(
                got_grads[rows, :],
                down_mat[cols, :],
                contract_cols,
                preferred_element_type=jnp.float32,
            ).astype(jnp.bfloat16)

        act_copies[g].start()

    def back_stage(g):
        pre_copies[g].wait_recv()
        act_copies[g].wait_recv()
        rows = pl.ds(g * GROUP * MOST, GROUP * MOST)

        @pl.loop(0, width // TILE)
        def _(c):
            cols = pl.ds(pl.multiple_of(c * TILE, TILE), TILE)
            up_cols = pl.ds(pl.multiple_of(width + c * TILE, TILE), TILE)

            def total(part, peer, where):
                return part[rows, where].astype(jnp.float32) + peer[rows, where].astype(jnp.float32)

            parts = local_grads(
                total(part_pre, peer_pre, cols),
                total(part_pre, peer_pre, up_cols),
                total(part_act, peer_act, cols),
            )
            hidden[rows, cols], grad_gate[rows, cols], grad_up[rows, cols] = parts

        @pl.loop(0, depth // TILE)
        def _(c):
            cols = pl.ds(pl.multiple_of(c * TILE, TILE), TILE)
            sums = lax.dot_general(
                grad_gate[rows, :],
                gate_mat[cols, :],
                contract_cols,
                preferred_element_type=jnp.float32,
            ) + lax.dot_general(
                grad_up[rows, :],
                up_mat[cols, :],
                contract_cols,
                preferred_element_type=jnp.float32,
            )
            slot_grad[rows, cols] = sums.astype(jnp.bfloat16)

        for k in members(g):
            if k == 0:
                returned[pl.ds(0, MOST), :] = slot_grad[pl.ds(0, MOST), :]
            else:
                back_copies[k].start()

    for load in loads:
        load.wait()
    near_groups = groups // 2
    for g in range(near_groups):
        pre_stage(g)
    for g in range(near_groups, groups):
        if g == near_groups:
            pre_stage(g)
            for early in range(near_groups):
                act_stage(early)
            act_stage(g)
            for early in range(near_groups):
                back_stage(early)
            back_stage(g)
        else:
            pre_stage(g)
            act_stage(g)
            back_stage(g)

    for copies in (tok_copies, grad_copies):
        for copy in copies.values():
            copy.wait_send()
    for g in range(groups):
        pre_copies[g].wait_send()
        act_copies[g].wait_send()
    for copy in back_copies.values():
        copy.wait()


def exchange(owners, send_tokens, send_grads, gate_mat, up_mat, down_mat):
    slots, depth = send_tokens.shape
    width = gate_mat.shape[1]
    groups = owners // GROUP
    bf16 = jnp.bfloat16
    wide = jax.ShapeDtypeStruct((slots, depth), bf16)
    thin = jax.ShapeDtypeStruct((slots, width), bf16)
    dma = pltpu.SemaphoreType.DMA
    return pl.pallas_call(
        functools.partial(exchange_kernel, owners),
        out_shape=(wide, wide, thin, thin, thin, wide),
        in_specs=[pl.BlockSpec(memory_space=pl.ANY)] * 5,
        out_specs=[pl.BlockSpec(memory_space=pltpu.VMEM)] * 6,
        scratch_shapes=[
            pltpu.VMEM((depth, width), bf16),
            pltpu.VMEM((depth, width), bf16),
            pltpu.VMEM((width, depth), bf16),
            pltpu.VMEM((slots, 2 * width), bf16),
            pltpu.VMEM((slots, width), bf16),
            pltpu.VMEM((slots, 2 * width), bf16),
            pltpu.VMEM((slots, width), bf16),
            pltpu.VMEM((slots, depth), bf16),
            dma((3,)),
            dma((2,)),
        ]
        + [dma((owners,))] * 4
        + [dma((groups,))] * 4
        + [dma((owners,))] * 2,
        compiler_params=pltpu.CompilerParams(
            collective_id=0, has_side_effects=True, vmem_limit_bytes=56 * 1024 * 1024
        ),
        cost_estimate=pl.CostEstimate(
            flops=10 * slots * depth * width,
            bytes_accessed=6 * depth * width + 10 * slots * depth + 6 * slots * width,
            transcendentals=slots * width,
        ),
        name="exchange",
    )(send_tokens, send_grads, gate_mat, up_mat, down_mat)


def fused_shards(tokens, out_grad, expert_ids, gate_probs, w_gate, w_up, w_down):
    tok_rows = tokens.shape[0]
    owners = lax.axis_size("expert")
    slots = owners * MOST
    me = lax.axis_index("expert").astype(jnp.int32)
    pick_ids = expert_ids.T.reshape(-1)
    onehot = (pick_ids[:, None] == jnp.arange(owners, dtype=jnp.int32)[None, :]).astype(jnp.int32)
    rank_in = jnp.sum((jnp.cumsum(onehot, axis=0) - 1) * onehot, axis=1)
    slot_of = ((pick_ids ^ me) * MOST + rank_in).reshape(2, tok_rows)
    slot_ids = jnp.arange(slots, dtype=jnp.int32)[:, None]
    first = slot_ids == slot_of[0][None, :]
    second = slot_ids == slot_of[1][None, :]
    placing = (first | second).astype(jnp.bfloat16)
    slot_prob = jnp.sum(
        jnp.where(first, gate_probs[:, 0][None, :], 0.0)
        + jnp.where(second, gate_probs[:, 1][None, :], 0.0),
        axis=1,
    )
    send_tokens = jnp.dot(placing, tokens, preferred_element_type=jnp.float32).astype(jnp.bfloat16)
    send_grads = (
        slot_prob[:, None] * jnp.dot(placing, out_grad, preferred_element_type=jnp.float32)
    ).astype(jnp.bfloat16)
    got_tokens, got_grads, hidden, grad_gate, grad_up, returned = exchange(
        owners, send_tokens, send_grads, w_gate[0], w_up[0], w_down[0]
    )

    def outer(left, right):
        return lax.dot_general(left, right, contract_rows, preferred_element_type=jnp.float32)[None]

    token_grad = lax.dot_general(
        placing, returned, contract_rows, preferred_element_type=jnp.float32
    ).astype(jnp.bfloat16)
    return (
        token_grad,
        outer(got_tokens, grad_gate),
        outer(got_tokens, grad_up),
        outer(hidden, got_grads),
    )


def fits_fused(mesh):
    owners = mesh.shape["expert"]
    return mesh.shape["dp"] == 2 and owners == 4 * GROUP


def solution(mesh):
    in_specs = (
        P("expert", "dp"),
        P("expert", "dp"),
        P("expert", None),
        P("expert", None),
        P("expert", "dp", None),
        P("expert", "dp", None),
        P("expert", None, "dp"),
    )
    out_specs = (
        P("expert", "dp"),
        P("expert", "dp", None),
        P("expert", "dp", None),
        P("expert", None, "dp"),
    )
    body = fused_shards if fits_fused(mesh) else shards
    return jax.shard_map(body, mesh=mesh, in_specs=in_specs, out_specs=out_specs, check_vma=False)
```

```python
import functools

import jax
import jax.numpy as jnp
from jax import lax
from jax.experimental import pallas as pl
from jax.experimental.pallas import tpu as pltpu
from jax.sharding import PartitionSpec as P

MOST = 32


contract_rows = (((0,), (0,)), ((), ()))
contract_cols = (((1,), (1,)), ((), ()))


def silu_parts(pre_gate):
    sigmoid_gate = jax.nn.sigmoid(pre_gate)
    return (pre_gate * sigmoid_gate, sigmoid_gate * (1.0 + pre_gate * (1.0 - sigmoid_gate)))


def local_grads(pre_gate, pre_up, grad_act):
    active, slope_gate = silu_parts(pre_gate)
    hidden = (active * pre_up).astype(jnp.bfloat16)
    grad_gate = (grad_act * pre_up * slope_gate).astype(jnp.bfloat16)
    grad_up = (grad_act * active).astype(jnp.bfloat16)
    return (hidden, grad_gate, grad_up)


def shards(tokens, out_grad, expert_ids, gate_probs, w_gate, w_up, w_down):
    tok_rows, slab_width = tokens.shape
    owners = lax.axis_size("expert")
    experts = owners * w_gate.shape[0]
    pick_ids = expert_ids.T.reshape(-1)
    onehot = (pick_ids[:, None] == jnp.arange(experts, dtype=jnp.int32)[None, :]).astype(jnp.int32)
    rank_in = jnp.sum((jnp.cumsum(onehot, axis=0) - 1) * onehot, axis=1)
    slot_of = pick_ids * MOST + rank_in
    placing = (jnp.arange(experts * MOST, dtype=jnp.int32)[:, None] == slot_of[None, :]).astype(
        jnp.bfloat16
    )
    row_pick = jnp.concatenate([tokens, tokens], axis=0)
    grad_pick = jnp.concatenate([out_grad, out_grad], axis=0)
    scaled = (gate_probs.T.reshape(-1)[:, None] * grad_pick.astype(jnp.float32)).astype(
        jnp.bfloat16
    )
    send_tokens = (
        jnp.dot(placing, row_pick, preferred_element_type=jnp.float32)
        .astype(jnp.bfloat16)
        .reshape(experts, MOST, slab_width)
    )
    send_grads = (
        jnp.dot(placing, scaled, preferred_element_type=jnp.float32)
        .astype(jnp.bfloat16)
        .reshape(experts, MOST, slab_width)
    )
    arrived_tokens, arrived_grads = (
        lax.all_to_all(send_tokens, "expert", split_axis=0, concat_axis=0, tiled=True),
        lax.all_to_all(send_grads, "expert", split_axis=0, concat_axis=0, tiled=True),
    )
    flat_tokens = arrived_tokens.reshape(-1, slab_width)
    flat_grads = arrived_grads.reshape(-1, slab_width)
    gate_mat = w_gate[0]
    up_mat = w_up[0]
    down_mat = w_down[0]
    part_gate = jnp.dot(flat_tokens, gate_mat, preferred_element_type=jnp.float32)
    part_up = jnp.dot(flat_tokens, up_mat, preferred_element_type=jnp.float32)
    part_act = lax.dot_general(
        flat_grads, down_mat, contract_cols, preferred_element_type=jnp.float32
    )
    pre_gate, pre_up, grad_act = (
        lax.psum(part_gate.astype(jnp.bfloat16), "dp").astype(jnp.float32),
        lax.psum(part_up.astype(jnp.bfloat16), "dp").astype(jnp.float32),
        lax.psum(part_act.astype(jnp.bfloat16), "dp").astype(jnp.float32),
    )
    hidden, grad_gate, grad_up = local_grads(pre_gate, pre_up, grad_act)
    slot_grad = lax.dot_general(
        grad_gate, gate_mat, contract_cols, preferred_element_type=jnp.float32
    )
    slot_grad = slot_grad + lax.dot_general(
        grad_up, up_mat, contract_cols, preferred_element_type=jnp.float32
    )
    gate_grads = lax.dot_general(
        flat_tokens, grad_gate, contract_rows, preferred_element_type=jnp.float32
    )[None]
    up_grads = lax.dot_general(
        flat_tokens, grad_up, contract_rows, preferred_element_type=jnp.float32
    )[None]
    down_grads = lax.dot_general(
        hidden, flat_grads, contract_rows, preferred_element_type=jnp.float32
    )[None]
    returned = lax.all_to_all(
        slot_grad.reshape(experts, MOST, slab_width).astype(jnp.bfloat16),
        "expert",
        split_axis=0,
        concat_axis=0,
        tiled=True,
    ).astype(jnp.float32)
    flat_back = returned.reshape(experts * MOST, slab_width)
    per_pick = jnp.take(flat_back, slot_of, axis=0)
    token_grad = (per_pick[:tok_rows] + per_pick[tok_rows:]).astype(jnp.bfloat16)
    return (token_grad, gate_grads, up_grads, down_grads)


GROUP = 4
TILE = 256


def partner_of(me, k, owners):
    result = 0
    bit = 1
    while bit < owners:
        digit = (me // bit) % 2
        result = result + bit * ((1 - digit) if k & bit else digit)
        bit *= 2
    return result


def exchange_kernel(
    owners,
    send_tokens,
    send_grads,
    w_gate,
    w_up,
    w_down,
    got_tokens,
    got_grads,
    hidden,
    grad_gate,
    grad_up,
    returned,
    last_a,
    last_b,
    last_c,
    last_d,
    gate_mat,
    up_mat,
    down_mat,
    part_pre,
    part_act,
    peer_pre,
    peer_act,
    slot_grad,
    load_sem,
    own_sem,
    tok_send,
    tok_recv,
    grad_send,
    grad_recv,
    pre_send,
    pre_recv,
    act_send,
    act_recv,
    back_send,
    back_recv,
):
    me = lax.axis_index("expert")
    other = 1 - lax.axis_index("dp")
    depth, width = w_gate.shape
    mesh_ids = pl.DeviceIdType.MESH

    loads = [
        pltpu.make_async_copy(source, target, load_sem.at[i])
        for i, (source, target) in enumerate(
            ((w_gate, gate_mat), (w_up, up_mat), (w_down, down_mat))
        )
    ]
    for load in loads:
        load.start()
    own = [
        pltpu.make_async_copy(source.at[pl.ds(0, MOST)], target.at[pl.ds(0, MOST)], own_sem.at[i])
        for i, (source, target) in enumerate(((send_tokens, got_tokens), (send_grads, got_grads)))
    ]
    for copy in own:
        copy.start()

    barrier = pltpu.get_barrier_semaphore()
    for k in range(1, owners):
        pl.semaphore_signal(
            barrier, inc=1, device_id={"expert": partner_of(me, k, owners)}, device_id_type=mesh_ids
        )
    pl.semaphore_signal(barrier, inc=1, device_id={"dp": other}, device_id_type=mesh_ids)
    pl.semaphore_wait(barrier, owners)

    def to_partner(k, source, target, send_sem, recv_sem):
        rows = pl.ds(k * MOST, MOST)
        return pltpu.make_async_remote_copy(
            src_ref=source.at[rows],
            dst_ref=target.at[rows],
            send_sem=send_sem.at[k],
            recv_sem=recv_sem.at[k],
            device_id={"expert": partner_of(me, k, owners)},
            device_id_type=mesh_ids,
        )

    def to_other(g, source, target, send_sem, recv_sem):
        rows = pl.ds(g * GROUP * MOST, GROUP * MOST)
        return pltpu.make_async_remote_copy(
            src_ref=source.at[rows],
            dst_ref=target.at[rows],
            send_sem=send_sem.at[g],
            recv_sem=recv_sem.at[g],
            device_id={"dp": other},
            device_id_type=mesh_ids,
        )

    groups = owners // GROUP
    tok_copies = {
        k: to_partner(k, send_tokens, got_tokens, tok_send, tok_recv) for k in range(1, owners)
    }
    grad_copies = {
        k: to_partner(k, send_grads, got_grads, grad_send, grad_recv) for k in range(1, owners)
    }
    pre_copies = [to_other(g, part_pre, peer_pre, pre_send, pre_recv) for g in range(groups)]
    act_copies = [to_other(g, part_act, peer_act, act_send, act_recv) for g in range(groups)]
    back_copies = {
        k: to_partner(k, slot_grad, returned, back_send, back_recv)
        for k in range(1, owners - GROUP)
    }
    last = (last_a, last_b, last_c, last_d)

    half = owners // 2
    near = list(range(1, half))
    far = list(range(half, owners))
    for copies in (tok_copies, grad_copies):
        for i in range(GROUP):
            copies[far[i]].start()
            for k in near[2 * i : 2 * i + 2]:
                copies[k].start()
    for first in range(GROUP, half, GROUP):
        for copies in (tok_copies, grad_copies):
            for k in far[first : first + GROUP]:
                copies[k].start()

    def members(g):
        return range(g * GROUP, (g + 1) * GROUP)

    def arrive(g, copies, own_copy):
        for k in members(g):
            if k == 0:
                own_copy.wait()
            else:
                copies[k].wait_recv()

    def pre_stage(g):
        arrive(g, tok_copies, own[0])
        rows = pl.ds(g * GROUP * MOST, GROUP * MOST)

        @pl.loop(0, width // TILE)
        def _(c):
            cols = pl.ds(pl.multiple_of(c * TILE, TILE), TILE)
            up_cols = pl.ds(pl.multiple_of(width + c * TILE, TILE), TILE)
            block = got_tokens[rows, :]
            part_pre[rows, cols] = jnp.dot(
                block, gate_mat[:, cols], preferred_element_type=jnp.float32
            ).astype(jnp.bfloat16)
            part_pre[rows, up_cols] = jnp.dot(
                block, up_mat[:, cols], preferred_element_type=jnp.float32
            ).astype(jnp.bfloat16)

        pre_copies[g].start()

    def act_stage(g):
        rows = pl.ds(g * GROUP * MOST, GROUP * MOST)

        @pl.loop(0, width // TILE)
        def _(c):
            cols = pl.ds(pl.multiple_of(c * TILE, TILE), TILE)
            part_act[rows, cols] = lax.dot_general(
                got_grads[rows, :],
                down_mat[cols, :],
                contract_cols,
                preferred_element_type=jnp.float32,
            ).astype(jnp.bfloat16)

        act_copies[g].start()

    def back_stage(g):
        pre_copies[g].wait_recv()
        act_copies[g].wait_recv()
        rows = pl.ds(g * GROUP * MOST, GROUP * MOST)

        @pl.loop(0, width // TILE)
        def _(c):
            cols = pl.ds(pl.multiple_of(c * TILE, TILE), TILE)
            up_cols = pl.ds(pl.multiple_of(width + c * TILE, TILE), TILE)

            def total(part, peer, where):
                return part[rows, where].astype(jnp.float32) + peer[rows, where].astype(jnp.float32)

            parts = local_grads(
                total(part_pre, peer_pre, cols),
                total(part_pre, peer_pre, up_cols),
                total(part_act, peer_act, cols),
            )
            hidden[rows, cols], grad_gate[rows, cols], grad_up[rows, cols] = parts

        @pl.loop(0, depth // TILE)
        def _(c):
            cols = pl.ds(pl.multiple_of(c * TILE, TILE), TILE)
            sums = lax.dot_general(
                grad_gate[rows, :],
                gate_mat[cols, :],
                contract_cols,
                preferred_element_type=jnp.float32,
            ) + lax.dot_general(
                grad_up[rows, :],
                up_mat[cols, :],
                contract_cols,
                preferred_element_type=jnp.float32,
            )
            sums = sums.astype(jnp.bfloat16)
            if g < groups - 1:
                slot_grad[rows, cols] = sums
            else:
                for i in range(GROUP):
                    last[i][:, cols] = sums[i * MOST : (i + 1) * MOST]

    def send_back(g):
        for k in members(g):
            if k == 0:
                returned[pl.ds(0, MOST), :] = slot_grad[pl.ds(0, MOST), :]
            else:
                back_copies[k].start()

    for load in loads:
        load.wait()
    near_groups = groups // 2
    for g in range(near_groups + 1):
        pre_stage(g)
    for g in range(near_groups + 1):
        arrive(g, grad_copies, own[1])
        act_stage(g)
    for g in range(near_groups):
        back_stage(g)
        send_back(g)
    back_stage(near_groups)
    pre_stage(groups - 1)
    arrive(groups - 1, grad_copies, own[1])
    send_back(near_groups)
    act_stage(groups - 1)
    back_stage(groups - 1)

    for copies in (tok_copies, grad_copies):
        for copy in copies.values():
            copy.wait_send()
    for g in range(groups):
        pre_copies[g].wait_send()
        act_copies[g].wait_send()
    for copy in back_copies.values():
        copy.wait()


def exchange(owners, send_tokens, send_grads, gate_mat, up_mat, down_mat):
    slots, depth = send_tokens.shape
    width = gate_mat.shape[1]
    groups = owners // GROUP
    bf16 = jnp.bfloat16
    wide = jax.ShapeDtypeStruct((slots, depth), bf16)
    back = jax.ShapeDtypeStruct((slots - GROUP * MOST, depth), bf16)
    piece = jax.ShapeDtypeStruct((MOST, depth), bf16)
    thin = jax.ShapeDtypeStruct((slots, width), bf16)
    dma = pltpu.SemaphoreType.DMA
    return pl.pallas_call(
        functools.partial(exchange_kernel, owners),
        out_shape=(wide, wide, thin, thin, thin, back) + (piece,) * GROUP,
        in_specs=[pl.BlockSpec(memory_space=pl.ANY)] * 5,
        out_specs=[pl.BlockSpec(memory_space=pltpu.VMEM)] * (6 + GROUP),
        scratch_shapes=[
            pltpu.VMEM((depth, width), bf16),
            pltpu.VMEM((depth, width), bf16),
            pltpu.VMEM((width, depth), bf16),
            pltpu.VMEM((slots, 2 * width), bf16),
            pltpu.VMEM((slots, width), bf16),
            pltpu.VMEM((slots, 2 * width), bf16),
            pltpu.VMEM((slots, width), bf16),
            pltpu.VMEM((slots - GROUP * MOST, depth), bf16),
            dma((3,)),
            dma((2,)),
        ]
        + [dma((owners,))] * 4
        + [dma((groups,))] * 4
        + [dma((owners - GROUP,))] * 2,
        compiler_params=pltpu.CompilerParams(
            collective_id=0, has_side_effects=True, vmem_limit_bytes=56 * 1024 * 1024
        ),
        cost_estimate=pl.CostEstimate(
            flops=10 * slots * depth * width,
            bytes_accessed=6 * depth * width + 10 * slots * depth + 6 * slots * width,
            transcendentals=slots * width,
        ),
        name="exchange",
    )(send_tokens, send_grads, gate_mat, up_mat, down_mat)


def fused_shards(tokens, out_grad, expert_ids, gate_probs, w_gate, w_up, w_down):
    tok_rows = tokens.shape[0]
    owners = lax.axis_size("expert")
    slots = owners * MOST
    me = lax.axis_index("expert").astype(jnp.int32)
    pick_ids = expert_ids.T.reshape(-1)
    onehot = (pick_ids[:, None] == jnp.arange(owners, dtype=jnp.int32)[None, :]).astype(jnp.int32)
    rank_in = jnp.sum((jnp.cumsum(onehot, axis=0) - 1) * onehot, axis=1)
    slot_of = ((pick_ids ^ me) * MOST + rank_in).reshape(2, tok_rows)
    slot_ids = jnp.arange(slots, dtype=jnp.int32)[:, None]
    first = slot_ids == slot_of[0][None, :]
    second = slot_ids == slot_of[1][None, :]
    placing = (first | second).astype(jnp.bfloat16)
    slot_prob = jnp.sum(
        jnp.where(first, gate_probs[:, 0][None, :], 0.0)
        + jnp.where(second, gate_probs[:, 1][None, :], 0.0),
        axis=1,
    )
    send_tokens = jnp.dot(placing, tokens, preferred_element_type=jnp.float32).astype(jnp.bfloat16)
    send_grads = (
        slot_prob[:, None] * jnp.dot(placing, out_grad, preferred_element_type=jnp.float32)
    ).astype(jnp.bfloat16)
    got_tokens, got_grads, hidden, grad_gate, grad_up, returned, *last = exchange(
        owners, send_tokens, send_grads, w_gate[0], w_up[0], w_down[0]
    )

    early = slots - GROUP * MOST
    last = [
        lax.ppermute(rows, "expert", [(i, i ^ (owners - GROUP + k)) for i in range(owners)])
        for k, rows in enumerate(last)
    ]

    def outer(left, right):
        return lax.dot_general(left, right, contract_rows, preferred_element_type=jnp.float32)[None]

    token_grad = lax.dot_general(
        placing[:early], returned, contract_rows, preferred_element_type=jnp.float32
    )
    token_grad = token_grad + lax.dot_general(
        placing[early:],
        jnp.concatenate(last, axis=0),
        contract_rows,
        preferred_element_type=jnp.float32,
    )
    token_grad = token_grad.astype(jnp.bfloat16)
    return (
        token_grad,
        outer(got_tokens, grad_gate),
        outer(got_tokens, grad_up),
        outer(hidden, got_grads),
    )


def fits_fused(mesh):
    owners = mesh.shape["expert"]
    return mesh.shape["dp"] == 2 and owners == 4 * GROUP


def solution(mesh):
    in_specs = (
        P("expert", "dp"),
        P("expert", "dp"),
        P("expert", None),
        P("expert", None),
        P("expert", "dp", None),
        P("expert", "dp", None),
        P("expert", None, "dp"),
    )
    out_specs = (
        P("expert", "dp"),
        P("expert", "dp", None),
        P("expert", "dp", None),
        P("expert", None, "dp"),
    )
    body = fused_shards if fits_fused(mesh) else shards
    return jax.shard_map(body, mesh=mesh, in_specs=in_specs, out_specs=out_specs, check_vma=False)
```

```python
import functools

import jax
import jax.numpy as jnp
from jax import lax
from jax.experimental import pallas as pl
from jax.experimental.pallas import tpu as pltpu
from jax.sharding import PartitionSpec as P

MOST = 32


contract_rows = (((0,), (0,)), ((), ()))
contract_cols = (((1,), (1,)), ((), ()))


def silu_parts(pre_gate):
    sigmoid_gate = jax.nn.sigmoid(pre_gate)
    return (pre_gate * sigmoid_gate, sigmoid_gate * (1.0 + pre_gate * (1.0 - sigmoid_gate)))


def local_grads(pre_gate, pre_up, grad_act):
    active, slope_gate = silu_parts(pre_gate)
    hidden = (active * pre_up).astype(jnp.bfloat16)
    grad_gate = (grad_act * pre_up * slope_gate).astype(jnp.bfloat16)
    grad_up = (grad_act * active).astype(jnp.bfloat16)
    return (hidden, grad_gate, grad_up)


def shards(tokens, out_grad, expert_ids, gate_probs, w_gate, w_up, w_down):
    tok_rows, slab_width = tokens.shape
    owners = lax.axis_size("expert")
    experts = owners * w_gate.shape[0]
    pick_ids = expert_ids.T.reshape(-1)
    onehot = (pick_ids[:, None] == jnp.arange(experts, dtype=jnp.int32)[None, :]).astype(jnp.int32)
    rank_in = jnp.sum((jnp.cumsum(onehot, axis=0) - 1) * onehot, axis=1)
    slot_of = pick_ids * MOST + rank_in
    placing = (jnp.arange(experts * MOST, dtype=jnp.int32)[:, None] == slot_of[None, :]).astype(
        jnp.bfloat16
    )
    row_pick = jnp.concatenate([tokens, tokens], axis=0)
    grad_pick = jnp.concatenate([out_grad, out_grad], axis=0)
    scaled = (gate_probs.T.reshape(-1)[:, None] * grad_pick.astype(jnp.float32)).astype(
        jnp.bfloat16
    )
    send_tokens = (
        jnp.dot(placing, row_pick, preferred_element_type=jnp.float32)
        .astype(jnp.bfloat16)
        .reshape(experts, MOST, slab_width)
    )
    send_grads = (
        jnp.dot(placing, scaled, preferred_element_type=jnp.float32)
        .astype(jnp.bfloat16)
        .reshape(experts, MOST, slab_width)
    )
    arrived_tokens, arrived_grads = (
        lax.all_to_all(send_tokens, "expert", split_axis=0, concat_axis=0, tiled=True),
        lax.all_to_all(send_grads, "expert", split_axis=0, concat_axis=0, tiled=True),
    )
    flat_tokens = arrived_tokens.reshape(-1, slab_width)
    flat_grads = arrived_grads.reshape(-1, slab_width)
    gate_mat = w_gate[0]
    up_mat = w_up[0]
    down_mat = w_down[0]
    part_gate = jnp.dot(flat_tokens, gate_mat, preferred_element_type=jnp.float32)
    part_up = jnp.dot(flat_tokens, up_mat, preferred_element_type=jnp.float32)
    part_act = lax.dot_general(
        flat_grads, down_mat, contract_cols, preferred_element_type=jnp.float32
    )
    pre_gate, pre_up, grad_act = (
        lax.psum(part_gate.astype(jnp.bfloat16), "dp").astype(jnp.float32),
        lax.psum(part_up.astype(jnp.bfloat16), "dp").astype(jnp.float32),
        lax.psum(part_act.astype(jnp.bfloat16), "dp").astype(jnp.float32),
    )
    hidden, grad_gate, grad_up = local_grads(pre_gate, pre_up, grad_act)
    slot_grad = lax.dot_general(
        grad_gate, gate_mat, contract_cols, preferred_element_type=jnp.float32
    )
    slot_grad = slot_grad + lax.dot_general(
        grad_up, up_mat, contract_cols, preferred_element_type=jnp.float32
    )
    gate_grads = lax.dot_general(
        flat_tokens, grad_gate, contract_rows, preferred_element_type=jnp.float32
    )[None]
    up_grads = lax.dot_general(
        flat_tokens, grad_up, contract_rows, preferred_element_type=jnp.float32
    )[None]
    down_grads = lax.dot_general(
        hidden, flat_grads, contract_rows, preferred_element_type=jnp.float32
    )[None]
    returned = lax.all_to_all(
        slot_grad.reshape(experts, MOST, slab_width).astype(jnp.bfloat16),
        "expert",
        split_axis=0,
        concat_axis=0,
        tiled=True,
    ).astype(jnp.float32)
    flat_back = returned.reshape(experts * MOST, slab_width)
    per_pick = jnp.take(flat_back, slot_of, axis=0)
    token_grad = (per_pick[:tok_rows] + per_pick[tok_rows:]).astype(jnp.bfloat16)
    return (token_grad, gate_grads, up_grads, down_grads)


GROUP = 4
TILE = 256


def partner_of(me, k, owners):
    result = 0
    bit = 1
    while bit < owners:
        digit = (me // bit) % 2
        result = result + bit * ((1 - digit) if k & bit else digit)
        bit *= 2
    return result


def exchange_kernel(
    owners,
    send_tokens,
    send_grads,
    w_gate,
    w_up,
    w_down,
    got_tokens,
    got_grads,
    hidden,
    grad_gate,
    grad_up,
    returned,
    last_a,
    last_b,
    last_c,
    last_d,
    gate_mat,
    up_mat,
    down_mat,
    part_pre,
    part_act,
    peer_pre,
    peer_act,
    slot_grad,
    load_sem,
    own_sem,
    tok_send,
    tok_recv,
    grad_send,
    grad_recv,
    pre_send,
    pre_recv,
    act_send,
    act_recv,
    back_send,
    back_recv,
):
    me = lax.axis_index("expert")
    other = 1 - lax.axis_index("dp")
    depth, width = w_gate.shape
    mesh_ids = pl.DeviceIdType.MESH

    loads = [
        pltpu.make_async_copy(source, target, load_sem.at[i])
        for i, (source, target) in enumerate(
            ((w_gate, gate_mat), (w_up, up_mat), (w_down, down_mat))
        )
    ]
    for load in loads:
        load.start()
    own = [
        pltpu.make_async_copy(source.at[pl.ds(0, MOST)], target.at[pl.ds(0, MOST)], own_sem.at[i])
        for i, (source, target) in enumerate(((send_tokens, got_tokens), (send_grads, got_grads)))
    ]
    for copy in own:
        copy.start()

    barrier = pltpu.get_barrier_semaphore()
    for k in range(1, owners):
        pl.semaphore_signal(
            barrier, inc=1, device_id={"expert": partner_of(me, k, owners)}, device_id_type=mesh_ids
        )
    pl.semaphore_signal(barrier, inc=1, device_id={"dp": other}, device_id_type=mesh_ids)
    pl.semaphore_wait(barrier, owners)

    def to_partner(k, source, target, send_sem, recv_sem):
        rows = pl.ds(k * MOST, MOST)
        return pltpu.make_async_remote_copy(
            src_ref=source.at[rows],
            dst_ref=target.at[rows],
            send_sem=send_sem.at[k],
            recv_sem=recv_sem.at[k],
            device_id={"expert": partner_of(me, k, owners)},
            device_id_type=mesh_ids,
        )

    def to_other(g, source, target, send_sem, recv_sem):
        rows = pl.ds(g * GROUP * MOST, GROUP * MOST)
        return pltpu.make_async_remote_copy(
            src_ref=source.at[rows],
            dst_ref=target.at[rows],
            send_sem=send_sem.at[g],
            recv_sem=recv_sem.at[g],
            device_id={"dp": other},
            device_id_type=mesh_ids,
        )

    groups = owners // GROUP
    tok_copies = {
        k: to_partner(k, send_tokens, got_tokens, tok_send, tok_recv) for k in range(1, owners)
    }
    grad_copies = {
        k: to_partner(k, send_grads, got_grads, grad_send, grad_recv) for k in range(1, owners)
    }
    pre_copies = [to_other(g, part_pre, peer_pre, pre_send, pre_recv) for g in range(groups)]
    act_copies = [to_other(g, part_act, peer_act, act_send, act_recv) for g in range(groups)]
    back_copies = {
        k: to_partner(k, slot_grad, returned, back_send, back_recv)
        for k in range(1, owners - GROUP)
    }
    last = (last_a, last_b, last_c, last_d)

    half = owners // 2
    near = list(range(1, half))
    far = list(range(half, owners))
    for copies in (tok_copies, grad_copies):
        for i in range(GROUP):
            copies[far[i]].start()
            for k in near[2 * i : 2 * i + 2]:
                copies[k].start()
    for first in range(GROUP, half, GROUP):
        for copies in (tok_copies, grad_copies):
            for k in far[first : first + GROUP]:
                copies[k].start()

    def members(g):
        return range(g * GROUP, (g + 1) * GROUP)

    def arrive(g, copies, own_copy):
        for k in members(g):
            if k == 0:
                own_copy.wait()
            else:
                copies[k].wait_recv()

    def pre_stage(g):
        arrive(g, tok_copies, own[0])
        rows = pl.ds(g * GROUP * MOST, GROUP * MOST)

        @pl.loop(0, width // TILE)
        def _(c):
            cols = pl.ds(pl.multiple_of(c * TILE, TILE), TILE)
            up_cols = pl.ds(pl.multiple_of(width + c * TILE, TILE), TILE)
            block = got_tokens[rows, :]
            part_pre[rows, cols] = jnp.dot(
                block, gate_mat[:, cols], preferred_element_type=jnp.float32
            ).astype(jnp.bfloat16)
            part_pre[rows, up_cols] = jnp.dot(
                block, up_mat[:, cols], preferred_element_type=jnp.float32
            ).astype(jnp.bfloat16)

        pre_copies[g].start()

    def act_stage(g):
        rows = pl.ds(g * GROUP * MOST, GROUP * MOST)

        @pl.loop(0, width // TILE)
        def _(c):
            cols = pl.ds(pl.multiple_of(c * TILE, TILE), TILE)
            part_act[rows, cols] = lax.dot_general(
                got_grads[rows, :],
                down_mat[cols, :],
                contract_cols,
                preferred_element_type=jnp.float32,
            ).astype(jnp.bfloat16)

        act_copies[g].start()

    def back_stage(g):
        pre_copies[g].wait_recv()
        act_copies[g].wait_recv()
        rows = pl.ds(g * GROUP * MOST, GROUP * MOST)

        @pl.loop(0, width // TILE)
        def _(c):
            cols = pl.ds(pl.multiple_of(c * TILE, TILE), TILE)
            up_cols = pl.ds(pl.multiple_of(width + c * TILE, TILE), TILE)

            def total(part, peer, where):
                return part[rows, where].astype(jnp.float32) + peer[rows, where].astype(jnp.float32)

            parts = local_grads(
                total(part_pre, peer_pre, cols),
                total(part_pre, peer_pre, up_cols),
                total(part_act, peer_act, cols),
            )
            hidden[rows, cols], grad_gate[rows, cols], grad_up[rows, cols] = parts

        @pl.loop(0, depth // TILE)
        def _(c):
            cols = pl.ds(pl.multiple_of(c * TILE, TILE), TILE)
            sums = lax.dot_general(
                grad_gate[rows, :],
                gate_mat[cols, :],
                contract_cols,
                preferred_element_type=jnp.float32,
            ) + lax.dot_general(
                grad_up[rows, :],
                up_mat[cols, :],
                contract_cols,
                preferred_element_type=jnp.float32,
            )
            sums = sums.astype(jnp.bfloat16)
            if g < groups - 1:
                slot_grad[rows, cols] = sums
            else:
                for i in range(GROUP):
                    last[i][:, cols] = sums[i * MOST : (i + 1) * MOST]

    def send_back(rows):
        for k in rows:
            if k == 0:
                returned[pl.ds(0, MOST), :] = slot_grad[pl.ds(0, MOST), :]
            else:
                back_copies[k].start()

    for load in loads:
        load.wait()
    near_groups = groups // 2
    for g in range(near_groups + 1):
        pre_stage(g)
    for g in range(near_groups + 1):
        arrive(g, grad_copies, own[1])
        act_stage(g)
    for g in range(near_groups):
        back_stage(g)
        send_back(members(g))
    back_stage(near_groups)
    held = members(near_groups)[GROUP // 2 :]
    send_back(members(near_groups)[: GROUP // 2])
    pre_stage(groups - 1)
    arrive(groups - 1, grad_copies, own[1])
    send_back(held)
    act_stage(groups - 1)
    back_stage(groups - 1)

    for copies in (tok_copies, grad_copies):
        for copy in copies.values():
            copy.wait_send()
    for g in range(groups):
        pre_copies[g].wait_send()
        act_copies[g].wait_send()
    for copy in back_copies.values():
        copy.wait()


def exchange(owners, send_tokens, send_grads, gate_mat, up_mat, down_mat):
    slots, depth = send_tokens.shape
    width = gate_mat.shape[1]
    groups = owners // GROUP
    bf16 = jnp.bfloat16
    wide = jax.ShapeDtypeStruct((slots, depth), bf16)
    back = jax.ShapeDtypeStruct((slots - GROUP * MOST, depth), bf16)
    piece = jax.ShapeDtypeStruct((MOST, depth), bf16)
    thin = jax.ShapeDtypeStruct((slots, width), bf16)
    dma = pltpu.SemaphoreType.DMA
    return pl.pallas_call(
        functools.partial(exchange_kernel, owners),
        out_shape=(wide, wide, thin, thin, thin, back) + (piece,) * GROUP,
        in_specs=[pl.BlockSpec(memory_space=pl.ANY)] * 5,
        out_specs=[pl.BlockSpec(memory_space=pltpu.VMEM)] * (6 + GROUP),
        scratch_shapes=[
            pltpu.VMEM((depth, width), bf16),
            pltpu.VMEM((depth, width), bf16),
            pltpu.VMEM((width, depth), bf16),
            pltpu.VMEM((slots, 2 * width), bf16),
            pltpu.VMEM((slots, width), bf16),
            pltpu.VMEM((slots, 2 * width), bf16),
            pltpu.VMEM((slots, width), bf16),
            pltpu.VMEM((slots - GROUP * MOST, depth), bf16),
            dma((3,)),
            dma((2,)),
        ]
        + [dma((owners,))] * 4
        + [dma((groups,))] * 4
        + [dma((owners - GROUP,))] * 2,
        compiler_params=pltpu.CompilerParams(
            collective_id=0, has_side_effects=True, vmem_limit_bytes=56 * 1024 * 1024
        ),
        cost_estimate=pl.CostEstimate(
            flops=10 * slots * depth * width,
            bytes_accessed=6 * depth * width + 10 * slots * depth + 6 * slots * width,
            transcendentals=slots * width,
        ),
        name="exchange",
    )(send_tokens, send_grads, gate_mat, up_mat, down_mat)


def fused_shards(tokens, out_grad, expert_ids, gate_probs, w_gate, w_up, w_down):
    tok_rows = tokens.shape[0]
    owners = lax.axis_size("expert")
    slots = owners * MOST
    me = lax.axis_index("expert").astype(jnp.int32)
    pick_ids = expert_ids.T.reshape(-1)
    order = jnp.arange(2 * tok_rows, dtype=jnp.int32)
    earlier = (pick_ids[:, None] == pick_ids[None, :]) & (order[:, None] < order[None, :])
    rank_in = jnp.sum(earlier.astype(jnp.int32), axis=0)
    slot_of = ((pick_ids ^ me) * MOST + rank_in).reshape(2, tok_rows)
    slot_ids = jnp.arange(slots, dtype=jnp.int32)[:, None]
    first = slot_ids == slot_of[0][None, :]
    second = slot_ids == slot_of[1][None, :]
    placing = (first | second).astype(jnp.bfloat16)
    slot_prob = jnp.sum(
        jnp.where(first, gate_probs[:, 0][None, :], 0.0)
        + jnp.where(second, gate_probs[:, 1][None, :], 0.0),
        axis=1,
    )
    send_tokens = jnp.dot(placing, tokens, preferred_element_type=jnp.float32).astype(jnp.bfloat16)
    send_grads = (
        slot_prob[:, None] * jnp.dot(placing, out_grad, preferred_element_type=jnp.float32)
    ).astype(jnp.bfloat16)
    got_tokens, got_grads, hidden, grad_gate, grad_up, returned, *last = exchange(
        owners, send_tokens, send_grads, w_gate[0], w_up[0], w_down[0]
    )

    early = slots - GROUP * MOST
    last = [
        lax.ppermute(rows, "expert", [(i, i ^ (owners - GROUP + k)) for i in range(owners)])
        for k, rows in enumerate(last)
    ]

    def outer(left, right):
        return lax.dot_general(left, right, contract_rows, preferred_element_type=jnp.float32)[None]

    token_grad = lax.dot_general(
        placing[:early], returned, contract_rows, preferred_element_type=jnp.float32
    )
    token_grad = token_grad + lax.dot_general(
        placing[early:],
        jnp.concatenate(last, axis=0),
        contract_rows,
        preferred_element_type=jnp.float32,
    )
    token_grad = token_grad.astype(jnp.bfloat16)
    return (
        token_grad,
        outer(got_tokens, grad_gate),
        outer(got_tokens, grad_up),
        outer(hidden, got_grads),
    )


def fits_fused(mesh):
    owners = mesh.shape["expert"]
    return mesh.shape["dp"] == 2 and owners == 4 * GROUP


def solution(mesh):
    in_specs = (
        P("expert", "dp"),
        P("expert", "dp"),
        P("expert", None),
        P("expert", None),
        P("expert", "dp", None),
        P("expert", "dp", None),
        P("expert", None, "dp"),
    )
    out_specs = (
        P("expert", "dp"),
        P("expert", "dp", None),
        P("expert", "dp", None),
        P("expert", None, "dp"),
    )
    body = fused_shards if fits_fused(mesh) else shards
    return jax.shard_map(body, mesh=mesh, in_specs=in_specs, out_specs=out_specs, check_vma=False)
```

```python
import functools

import jax
import jax.numpy as jnp
from jax import lax
from jax.experimental import pallas as pl
from jax.experimental.pallas import tpu as pltpu
from jax.sharding import PartitionSpec as P

MOST = 32


contract_rows = (((0,), (0,)), ((), ()))
contract_cols = (((1,), (1,)), ((), ()))


def silu_parts(pre_gate):
    sigmoid_gate = jax.nn.sigmoid(pre_gate)
    return (pre_gate * sigmoid_gate, sigmoid_gate * (1.0 + pre_gate * (1.0 - sigmoid_gate)))


def local_grads(pre_gate, pre_up, grad_act):
    active, slope_gate = silu_parts(pre_gate)
    hidden = (active * pre_up).astype(jnp.bfloat16)
    grad_gate = (grad_act * pre_up * slope_gate).astype(jnp.bfloat16)
    grad_up = (grad_act * active).astype(jnp.bfloat16)
    return (hidden, grad_gate, grad_up)


def shards(tokens, out_grad, expert_ids, gate_probs, w_gate, w_up, w_down):
    tok_rows, slab_width = tokens.shape
    owners = lax.axis_size("expert")
    experts = owners * w_gate.shape[0]
    pick_ids = expert_ids.T.reshape(-1)
    onehot = (pick_ids[:, None] == jnp.arange(experts, dtype=jnp.int32)[None, :]).astype(jnp.int32)
    rank_in = jnp.sum((jnp.cumsum(onehot, axis=0) - 1) * onehot, axis=1)
    slot_of = pick_ids * MOST + rank_in
    placing = (jnp.arange(experts * MOST, dtype=jnp.int32)[:, None] == slot_of[None, :]).astype(
        jnp.bfloat16
    )
    row_pick = jnp.concatenate([tokens, tokens], axis=0)
    grad_pick = jnp.concatenate([out_grad, out_grad], axis=0)
    scaled = (gate_probs.T.reshape(-1)[:, None] * grad_pick.astype(jnp.float32)).astype(
        jnp.bfloat16
    )
    send_tokens = (
        jnp.dot(placing, row_pick, preferred_element_type=jnp.float32)
        .astype(jnp.bfloat16)
        .reshape(experts, MOST, slab_width)
    )
    send_grads = (
        jnp.dot(placing, scaled, preferred_element_type=jnp.float32)
        .astype(jnp.bfloat16)
        .reshape(experts, MOST, slab_width)
    )
    arrived_tokens, arrived_grads = (
        lax.all_to_all(send_tokens, "expert", split_axis=0, concat_axis=0, tiled=True),
        lax.all_to_all(send_grads, "expert", split_axis=0, concat_axis=0, tiled=True),
    )
    flat_tokens = arrived_tokens.reshape(-1, slab_width)
    flat_grads = arrived_grads.reshape(-1, slab_width)
    gate_mat = w_gate[0]
    up_mat = w_up[0]
    down_mat = w_down[0]
    part_gate = jnp.dot(flat_tokens, gate_mat, preferred_element_type=jnp.float32)
    part_up = jnp.dot(flat_tokens, up_mat, preferred_element_type=jnp.float32)
    part_act = lax.dot_general(
        flat_grads, down_mat, contract_cols, preferred_element_type=jnp.float32
    )
    pre_gate, pre_up, grad_act = (
        lax.psum(part_gate.astype(jnp.bfloat16), "dp").astype(jnp.float32),
        lax.psum(part_up.astype(jnp.bfloat16), "dp").astype(jnp.float32),
        lax.psum(part_act.astype(jnp.bfloat16), "dp").astype(jnp.float32),
    )
    hidden, grad_gate, grad_up = local_grads(pre_gate, pre_up, grad_act)
    slot_grad = lax.dot_general(
        grad_gate, gate_mat, contract_cols, preferred_element_type=jnp.float32
    )
    slot_grad = slot_grad + lax.dot_general(
        grad_up, up_mat, contract_cols, preferred_element_type=jnp.float32
    )
    gate_grads = lax.dot_general(
        flat_tokens, grad_gate, contract_rows, preferred_element_type=jnp.float32
    )[None]
    up_grads = lax.dot_general(
        flat_tokens, grad_up, contract_rows, preferred_element_type=jnp.float32
    )[None]
    down_grads = lax.dot_general(
        hidden, flat_grads, contract_rows, preferred_element_type=jnp.float32
    )[None]
    returned = lax.all_to_all(
        slot_grad.reshape(experts, MOST, slab_width).astype(jnp.bfloat16),
        "expert",
        split_axis=0,
        concat_axis=0,
        tiled=True,
    ).astype(jnp.float32)
    flat_back = returned.reshape(experts * MOST, slab_width)
    per_pick = jnp.take(flat_back, slot_of, axis=0)
    token_grad = (per_pick[:tok_rows] + per_pick[tok_rows:]).astype(jnp.bfloat16)
    return (token_grad, gate_grads, up_grads, down_grads)


GROUP = 4
TILE = 256


def partner_of(me, k, owners):
    result = 0
    bit = 1
    while bit < owners:
        digit = (me // bit) % 2
        result = result + bit * ((1 - digit) if k & bit else digit)
        bit *= 2
    return result


def exchange_kernel(
    owners,
    send_tokens,
    send_grads,
    w_gate,
    w_up,
    w_down,
    got_tokens,
    got_grads,
    hidden,
    grad_gate,
    grad_up,
    returned,
    last_a,
    last_b,
    last_c,
    last_d,
    gate_mat,
    up_mat,
    down_mat,
    part_pre,
    part_act,
    peer_pre,
    peer_act,
    slot_grad,
    load_sem,
    own_sem,
    tok_send,
    tok_recv,
    grad_send,
    grad_recv,
    pre_send,
    pre_recv,
    act_send,
    act_recv,
    back_send,
    back_recv,
):
    me = lax.axis_index("expert")
    other = 1 - lax.axis_index("dp")
    depth, width = w_gate.shape
    mesh_ids = pl.DeviceIdType.MESH

    loads = [
        pltpu.make_async_copy(source, target, load_sem.at[i])
        for i, (source, target) in enumerate(
            ((w_gate, gate_mat), (w_up, up_mat), (w_down, down_mat))
        )
    ]
    for load in loads:
        load.start()
    own = [
        pltpu.make_async_copy(source.at[pl.ds(0, MOST)], target.at[pl.ds(0, MOST)], own_sem.at[i])
        for i, (source, target) in enumerate(((send_tokens, got_tokens), (send_grads, got_grads)))
    ]
    for copy in own:
        copy.start()

    barrier = pltpu.get_barrier_semaphore()
    for k in range(1, owners):
        pl.semaphore_signal(
            barrier, inc=1, device_id={"expert": partner_of(me, k, owners)}, device_id_type=mesh_ids
        )
    pl.semaphore_signal(barrier, inc=1, device_id={"dp": other}, device_id_type=mesh_ids)
    pl.semaphore_wait(barrier, owners)

    def to_partner(k, source, target, send_sem, recv_sem):
        rows = pl.ds(k * MOST, MOST)
        return pltpu.make_async_remote_copy(
            src_ref=source.at[rows],
            dst_ref=target.at[rows],
            send_sem=send_sem.at[k],
            recv_sem=recv_sem.at[k],
            device_id={"expert": partner_of(me, k, owners)},
            device_id_type=mesh_ids,
        )

    def to_other(g, source, target, send_sem, recv_sem):
        rows = pl.ds(g * GROUP * MOST, GROUP * MOST)
        return pltpu.make_async_remote_copy(
            src_ref=source.at[rows],
            dst_ref=target.at[rows],
            send_sem=send_sem.at[g],
            recv_sem=recv_sem.at[g],
            device_id={"dp": other},
            device_id_type=mesh_ids,
        )

    groups = owners // GROUP
    tok_copies = {
        k: to_partner(k, send_tokens, got_tokens, tok_send, tok_recv) for k in range(1, owners)
    }
    grad_copies = {
        k: to_partner(k, send_grads, got_grads, grad_send, grad_recv) for k in range(1, owners)
    }
    pre_copies = [to_other(g, part_pre, peer_pre, pre_send, pre_recv) for g in range(groups)]
    act_copies = [to_other(g, part_act, peer_act, act_send, act_recv) for g in range(groups)]
    back_copies = {
        k: to_partner(k, slot_grad, returned, back_send, back_recv)
        for k in range(1, owners - GROUP)
    }
    last = (last_a, last_b, last_c, last_d)

    half = owners // 2
    near = list(range(1, half))
    far = list(range(half, owners))
    for copies in (tok_copies, grad_copies):
        for i in range(GROUP):
            copies[far[i]].start()
            for k in near[2 * i : 2 * i + 2]:
                copies[k].start()

    def members(g):
        return range(g * GROUP, (g + 1) * GROUP)

    def arrive(g, copies, own_copy):
        for k in members(g):
            if k == 0:
                own_copy.wait()
            else:
                copies[k].wait_recv()

    def pre_stage(g):
        arrive(g, tok_copies, own[0])
        rows = pl.ds(g * GROUP * MOST, GROUP * MOST)

        @pl.loop(0, width // TILE)
        def _(c):
            cols = pl.ds(pl.multiple_of(c * TILE, TILE), TILE)
            up_cols = pl.ds(pl.multiple_of(width + c * TILE, TILE), TILE)
            block = got_tokens[rows, :]
            part_pre[rows, cols] = jnp.dot(
                block, gate_mat[:, cols], preferred_element_type=jnp.float32
            ).astype(jnp.bfloat16)
            part_pre[rows, up_cols] = jnp.dot(
                block, up_mat[:, cols], preferred_element_type=jnp.float32
            ).astype(jnp.bfloat16)

        pre_copies[g].start()

    def act_stage(g):
        rows = pl.ds(g * GROUP * MOST, GROUP * MOST)

        @pl.loop(0, width // TILE)
        def _(c):
            cols = pl.ds(pl.multiple_of(c * TILE, TILE), TILE)
            part_act[rows, cols] = lax.dot_general(
                got_grads[rows, :],
                down_mat[cols, :],
                contract_cols,
                preferred_element_type=jnp.float32,
            ).astype(jnp.bfloat16)

        act_copies[g].start()

    def back_stage(g):
        pre_copies[g].wait_recv()
        act_copies[g].wait_recv()
        rows = pl.ds(g * GROUP * MOST, GROUP * MOST)

        @pl.loop(0, width // TILE)
        def _(c):
            cols = pl.ds(pl.multiple_of(c * TILE, TILE), TILE)
            up_cols = pl.ds(pl.multiple_of(width + c * TILE, TILE), TILE)

            def total(part, peer, where):
                return part[rows, where].astype(jnp.float32) + peer[rows, where].astype(jnp.float32)

            parts = local_grads(
                total(part_pre, peer_pre, cols),
                total(part_pre, peer_pre, up_cols),
                total(part_act, peer_act, cols),
            )
            hidden[rows, cols], grad_gate[rows, cols], grad_up[rows, cols] = parts

        @pl.loop(0, depth // TILE)
        def _(c):
            cols = pl.ds(pl.multiple_of(c * TILE, TILE), TILE)
            sums = lax.dot_general(
                grad_gate[rows, :],
                gate_mat[cols, :],
                contract_cols,
                preferred_element_type=jnp.float32,
            ) + lax.dot_general(
                grad_up[rows, :],
                up_mat[cols, :],
                contract_cols,
                preferred_element_type=jnp.float32,
            )
            sums = sums.astype(jnp.bfloat16)
            if g < groups - 1:
                slot_grad[rows, cols] = sums
            else:
                for i in range(GROUP):
                    last[i][:, cols] = sums[i * MOST : (i + 1) * MOST]

    def send_back(rows):
        for k in rows:
            if k == 0:
                returned[pl.ds(0, MOST), :] = slot_grad[pl.ds(0, MOST), :]
            else:
                back_copies[k].start()

    for load in loads:
        load.wait()
    near_groups = groups // 2
    for g in range(near_groups + 1):
        pre_stage(g)
    for k in far[GROUP:]:
        tok_copies[k].start()
    for g in range(near_groups + 1):
        arrive(g, grad_copies, own[1])
        act_stage(g)
    for k in far[GROUP:]:
        grad_copies[k].start()
    for g in range(near_groups):
        back_stage(g)
        send_back(members(g))
    back_stage(near_groups)
    held = members(near_groups)[GROUP // 2 :]
    send_back(members(near_groups)[: GROUP // 2])
    pre_stage(groups - 1)
    arrive(groups - 1, grad_copies, own[1])
    act_stage(groups - 1)
    send_back(held)
    back_stage(groups - 1)

    for copies in (tok_copies, grad_copies):
        for copy in copies.values():
            copy.wait_send()
    for g in range(groups):
        pre_copies[g].wait_send()
        act_copies[g].wait_send()
    for copy in back_copies.values():
        copy.wait()


def exchange(owners, send_tokens, send_grads, gate_mat, up_mat, down_mat):
    slots, depth = send_tokens.shape
    width = gate_mat.shape[1]
    groups = owners // GROUP
    bf16 = jnp.bfloat16
    wide = jax.ShapeDtypeStruct((slots, depth), bf16)
    back = jax.ShapeDtypeStruct((slots - GROUP * MOST, depth), bf16)
    piece = jax.ShapeDtypeStruct((MOST, depth), bf16)
    thin = jax.ShapeDtypeStruct((slots, width), bf16)
    dma = pltpu.SemaphoreType.DMA
    return pl.pallas_call(
        functools.partial(exchange_kernel, owners),
        out_shape=(wide, wide, thin, thin, thin, back) + (piece,) * GROUP,
        in_specs=[pl.BlockSpec(memory_space=pl.ANY)] * 5,
        out_specs=[pl.BlockSpec(memory_space=pltpu.VMEM)] * (6 + GROUP),
        scratch_shapes=[
            pltpu.VMEM((depth, width), bf16),
            pltpu.VMEM((depth, width), bf16),
            pltpu.VMEM((width, depth), bf16),
            pltpu.VMEM((slots, 2 * width), bf16),
            pltpu.VMEM((slots, width), bf16),
            pltpu.VMEM((slots, 2 * width), bf16),
            pltpu.VMEM((slots, width), bf16),
            pltpu.VMEM((slots - GROUP * MOST, depth), bf16),
            dma((3,)),
            dma((2,)),
        ]
        + [dma((owners,))] * 4
        + [dma((groups,))] * 4
        + [dma((owners - GROUP,))] * 2,
        compiler_params=pltpu.CompilerParams(
            collective_id=0, has_side_effects=True, vmem_limit_bytes=56 * 1024 * 1024
        ),
        cost_estimate=pl.CostEstimate(
            flops=10 * slots * depth * width,
            bytes_accessed=6 * depth * width + 10 * slots * depth + 6 * slots * width,
            transcendentals=slots * width,
        ),
        name="exchange",
    )(send_tokens, send_grads, gate_mat, up_mat, down_mat)


def fused_shards(tokens, out_grad, expert_ids, gate_probs, w_gate, w_up, w_down):
    tok_rows = tokens.shape[0]
    owners = lax.axis_size("expert")
    slots = owners * MOST
    me = lax.axis_index("expert").astype(jnp.int32)
    pick_ids = expert_ids.T.reshape(-1)
    order = jnp.arange(2 * tok_rows, dtype=jnp.int32)
    earlier = (pick_ids[:, None] == pick_ids[None, :]) & (order[:, None] < order[None, :])
    rank_in = jnp.sum(earlier.astype(jnp.int32), axis=0)
    slot_of = ((pick_ids ^ me) * MOST + rank_in).reshape(2, tok_rows)
    slot_ids = jnp.arange(slots, dtype=jnp.int32)[:, None]
    first = slot_ids == slot_of[0][None, :]
    second = slot_ids == slot_of[1][None, :]
    placing = (first | second).astype(jnp.bfloat16)
    slot_prob = jnp.sum(
        jnp.where(first, gate_probs[:, 0][None, :], 0.0)
        + jnp.where(second, gate_probs[:, 1][None, :], 0.0),
        axis=1,
    )
    send_tokens = jnp.dot(placing, tokens, preferred_element_type=jnp.float32).astype(jnp.bfloat16)
    send_grads = (
        slot_prob[:, None] * jnp.dot(placing, out_grad, preferred_element_type=jnp.float32)
    ).astype(jnp.bfloat16)
    got_tokens, got_grads, hidden, grad_gate, grad_up, returned, *last = exchange(
        owners, send_tokens, send_grads, w_gate[0], w_up[0], w_down[0]
    )

    early = slots - GROUP * MOST
    last = [
        lax.ppermute(rows, "expert", [(i, i ^ (owners - GROUP + k)) for i in range(owners)])
        for k, rows in enumerate(last)
    ]

    def outer(left, right):
        return lax.dot_general(left, right, contract_rows, preferred_element_type=jnp.float32)[None]

    token_grad = lax.dot_general(
        placing[:early], returned, contract_rows, preferred_element_type=jnp.float32
    )
    token_grad = token_grad + lax.dot_general(
        placing[early:],
        jnp.concatenate(last, axis=0),
        contract_rows,
        preferred_element_type=jnp.float32,
    )
    token_grad = token_grad.astype(jnp.bfloat16)
    return (
        token_grad,
        outer(got_tokens, grad_gate),
        outer(got_tokens, grad_up),
        outer(hidden, got_grads),
    )


def fits_fused(mesh):
    owners = mesh.shape["expert"]
    return mesh.shape["dp"] == 2 and owners == 4 * GROUP


def solution(mesh):
    in_specs = (
        P("expert", "dp"),
        P("expert", "dp"),
        P("expert", None),
        P("expert", None),
        P("expert", "dp", None),
        P("expert", "dp", None),
        P("expert", None, "dp"),
    )
    out_specs = (
        P("expert", "dp"),
        P("expert", "dp", None),
        P("expert", "dp", None),
        P("expert", None, "dp"),
    )
    body = fused_shards if fits_fused(mesh) else shards
    return jax.shard_map(body, mesh=mesh, in_specs=in_specs, out_specs=out_specs, check_vma=False)
```

```python
import functools

import jax
import jax.numpy as jnp
from jax import lax
from jax.experimental import pallas as pl
from jax.experimental.pallas import tpu as pltpu
from jax.sharding import PartitionSpec as P

MOST = 32


contract_rows = (((0,), (0,)), ((), ()))
contract_cols = (((1,), (1,)), ((), ()))


def silu_parts(pre_gate):
    sigmoid_gate = jax.nn.sigmoid(pre_gate)
    return (pre_gate * sigmoid_gate, sigmoid_gate * (1.0 + pre_gate * (1.0 - sigmoid_gate)))


def local_grads(pre_gate, pre_up, grad_act):
    active, slope_gate = silu_parts(pre_gate)
    hidden = (active * pre_up).astype(jnp.bfloat16)
    grad_gate = (grad_act * pre_up * slope_gate).astype(jnp.bfloat16)
    grad_up = (grad_act * active).astype(jnp.bfloat16)
    return (hidden, grad_gate, grad_up)


def shards(tokens, out_grad, expert_ids, gate_probs, w_gate, w_up, w_down):
    tok_rows, slab_width = tokens.shape
    owners = lax.axis_size("expert")
    experts = owners * w_gate.shape[0]
    pick_ids = expert_ids.T.reshape(-1)
    onehot = (pick_ids[:, None] == jnp.arange(experts, dtype=jnp.int32)[None, :]).astype(jnp.int32)
    rank_in = jnp.sum((jnp.cumsum(onehot, axis=0) - 1) * onehot, axis=1)
    slot_of = pick_ids * MOST + rank_in
    placing = (jnp.arange(experts * MOST, dtype=jnp.int32)[:, None] == slot_of[None, :]).astype(
        jnp.bfloat16
    )
    row_pick = jnp.concatenate([tokens, tokens], axis=0)
    grad_pick = jnp.concatenate([out_grad, out_grad], axis=0)
    scaled = (gate_probs.T.reshape(-1)[:, None] * grad_pick.astype(jnp.float32)).astype(
        jnp.bfloat16
    )
    send_tokens = (
        jnp.dot(placing, row_pick, preferred_element_type=jnp.float32)
        .astype(jnp.bfloat16)
        .reshape(experts, MOST, slab_width)
    )
    send_grads = (
        jnp.dot(placing, scaled, preferred_element_type=jnp.float32)
        .astype(jnp.bfloat16)
        .reshape(experts, MOST, slab_width)
    )
    arrived_tokens, arrived_grads = (
        lax.all_to_all(send_tokens, "expert", split_axis=0, concat_axis=0, tiled=True),
        lax.all_to_all(send_grads, "expert", split_axis=0, concat_axis=0, tiled=True),
    )
    flat_tokens = arrived_tokens.reshape(-1, slab_width)
    flat_grads = arrived_grads.reshape(-1, slab_width)
    gate_mat = w_gate[0]
    up_mat = w_up[0]
    down_mat = w_down[0]
    part_gate = jnp.dot(flat_tokens, gate_mat, preferred_element_type=jnp.float32)
    part_up = jnp.dot(flat_tokens, up_mat, preferred_element_type=jnp.float32)
    part_act = lax.dot_general(
        flat_grads, down_mat, contract_cols, preferred_element_type=jnp.float32
    )
    pre_gate, pre_up, grad_act = (
        lax.psum(part_gate.astype(jnp.bfloat16), "dp").astype(jnp.float32),
        lax.psum(part_up.astype(jnp.bfloat16), "dp").astype(jnp.float32),
        lax.psum(part_act.astype(jnp.bfloat16), "dp").astype(jnp.float32),
    )
    hidden, grad_gate, grad_up = local_grads(pre_gate, pre_up, grad_act)
    slot_grad = lax.dot_general(
        grad_gate, gate_mat, contract_cols, preferred_element_type=jnp.float32
    )
    slot_grad = slot_grad + lax.dot_general(
        grad_up, up_mat, contract_cols, preferred_element_type=jnp.float32
    )
    gate_grads = lax.dot_general(
        flat_tokens, grad_gate, contract_rows, preferred_element_type=jnp.float32
    )[None]
    up_grads = lax.dot_general(
        flat_tokens, grad_up, contract_rows, preferred_element_type=jnp.float32
    )[None]
    down_grads = lax.dot_general(
        hidden, flat_grads, contract_rows, preferred_element_type=jnp.float32
    )[None]
    returned = lax.all_to_all(
        slot_grad.reshape(experts, MOST, slab_width).astype(jnp.bfloat16),
        "expert",
        split_axis=0,
        concat_axis=0,
        tiled=True,
    ).astype(jnp.float32)
    flat_back = returned.reshape(experts * MOST, slab_width)
    per_pick = jnp.take(flat_back, slot_of, axis=0)
    token_grad = (per_pick[:tok_rows] + per_pick[tok_rows:]).astype(jnp.bfloat16)
    return (token_grad, gate_grads, up_grads, down_grads)


GROUP = 4
TILE = 256


def partner_of(me, k, owners):
    result = 0
    bit = 1
    while bit < owners:
        digit = (me // bit) % 2
        result = result + bit * ((1 - digit) if k & bit else digit)
        bit *= 2
    return result


def exchange_kernel(
    owners,
    send_tokens,
    send_grads,
    w_gate,
    w_up,
    w_down,
    got_tokens,
    got_grads,
    hidden,
    grad_gate,
    grad_up,
    returned,
    last_a,
    last_b,
    last_c,
    last_d,
    gate_mat,
    up_mat,
    down_mat,
    part_pre,
    part_act,
    peer_pre,
    peer_act,
    slot_grad,
    load_sem,
    own_sem,
    tok_send,
    tok_recv,
    grad_send,
    grad_recv,
    pre_send,
    pre_recv,
    act_send,
    act_recv,
    back_send,
    back_recv,
):
    me = lax.axis_index("expert")
    other = 1 - lax.axis_index("dp")
    depth, width = w_gate.shape
    mesh_ids = pl.DeviceIdType.MESH

    loads = [
        pltpu.make_async_copy(source, target, load_sem.at[i])
        for i, (source, target) in enumerate(
            ((w_gate, gate_mat), (w_up, up_mat), (w_down, down_mat))
        )
    ]
    for load in loads:
        load.start()
    own = [
        pltpu.make_async_copy(source.at[pl.ds(0, MOST)], target.at[pl.ds(0, MOST)], own_sem.at[i])
        for i, (source, target) in enumerate(((send_tokens, got_tokens), (send_grads, got_grads)))
    ]
    for copy in own:
        copy.start()

    barrier = pltpu.get_barrier_semaphore()
    for k in range(1, owners):
        pl.semaphore_signal(
            barrier, inc=1, device_id={"expert": partner_of(me, k, owners)}, device_id_type=mesh_ids
        )
    pl.semaphore_signal(barrier, inc=1, device_id={"dp": other}, device_id_type=mesh_ids)
    pl.semaphore_wait(barrier, owners)

    def to_partner(k, source, target, send_sem, recv_sem):
        rows = pl.ds(k * MOST, MOST)
        return pltpu.make_async_remote_copy(
            src_ref=source.at[rows],
            dst_ref=target.at[rows],
            send_sem=send_sem.at[k],
            recv_sem=recv_sem.at[k],
            device_id={"expert": partner_of(me, k, owners)},
            device_id_type=mesh_ids,
        )

    def to_other(g, source, target, send_sem, recv_sem):
        rows = pl.ds(g * GROUP * MOST, GROUP * MOST)
        return pltpu.make_async_remote_copy(
            src_ref=source.at[rows],
            dst_ref=target.at[rows],
            send_sem=send_sem.at[g],
            recv_sem=recv_sem.at[g],
            device_id={"dp": other},
            device_id_type=mesh_ids,
        )

    groups = owners // GROUP
    tok_copies = {
        k: to_partner(k, send_tokens, got_tokens, tok_send, tok_recv) for k in range(1, owners)
    }
    grad_copies = {
        k: to_partner(k, send_grads, got_grads, grad_send, grad_recv) for k in range(1, owners)
    }
    pre_copies = [to_other(g, part_pre, peer_pre, pre_send, pre_recv) for g in range(groups)]
    act_copies = [to_other(g, part_act, peer_act, act_send, act_recv) for g in range(groups)]
    back_copies = {
        k: to_partner(k, slot_grad, returned, back_send, back_recv)
        for k in range(1, owners - GROUP)
    }
    last = (last_a, last_b, last_c, last_d)

    half = owners // 2
    near = list(range(1, half))
    far = list(range(half, owners))
    for copies in (tok_copies, grad_copies):
        for i in range(GROUP):
            copies[far[i]].start()
            for k in near[2 * i : 2 * i + 2]:
                copies[k].start()

    for first in range(GROUP, half, GROUP):
        for copies in (tok_copies, grad_copies):
            for k in far[first : first + GROUP]:
                copies[k].start()

    def members(g):
        return range(g * GROUP, (g + 1) * GROUP)

    def arrive(g, copies, own_copy):
        for k in members(g):
            if k == 0:
                own_copy.wait()
            else:
                copies[k].wait_recv()

    def pre_stage(g, span=1):
        for each in range(g, g + span):
            arrive(each, tok_copies, own[0])
        rows = pl.ds(g * GROUP * MOST, span * GROUP * MOST)

        @pl.loop(0, width // TILE)
        def _(c):
            cols = pl.ds(pl.multiple_of(c * TILE, TILE), TILE)
            up_cols = pl.ds(pl.multiple_of(width + c * TILE, TILE), TILE)
            block = got_tokens[rows, :]
            part_pre[rows, cols] = jnp.dot(
                block, gate_mat[:, cols], preferred_element_type=jnp.float32
            ).astype(jnp.bfloat16)
            part_pre[rows, up_cols] = jnp.dot(
                block, up_mat[:, cols], preferred_element_type=jnp.float32
            ).astype(jnp.bfloat16)

        for each in range(g, g + span):
            pre_copies[each].start()

    def act_stage(g, span=1):
        for each in range(g, g + span):
            arrive(each, grad_copies, own[1])
        rows = pl.ds(g * GROUP * MOST, span * GROUP * MOST)

        @pl.loop(0, width // TILE)
        def _(c):
            cols = pl.ds(pl.multiple_of(c * TILE, TILE), TILE)
            part_act[rows, cols] = lax.dot_general(
                got_grads[rows, :],
                down_mat[cols, :],
                contract_cols,
                preferred_element_type=jnp.float32,
            ).astype(jnp.bfloat16)

        for each in range(g, g + span):
            act_copies[each].start()

    def back_stage(g, span=1):
        for each in range(g, g + span):
            pre_copies[each].wait_recv()
            act_copies[each].wait_recv()
        rows = pl.ds(g * GROUP * MOST, span * GROUP * MOST)

        @pl.loop(0, width // TILE)
        def _(c):
            cols = pl.ds(pl.multiple_of(c * TILE, TILE), TILE)
            up_cols = pl.ds(pl.multiple_of(width + c * TILE, TILE), TILE)

            def total(part, peer, where):
                return part[rows, where].astype(jnp.float32) + peer[rows, where].astype(jnp.float32)

            parts = local_grads(
                total(part_pre, peer_pre, cols),
                total(part_pre, peer_pre, up_cols),
                total(part_act, peer_act, cols),
            )
            hidden[rows, cols], grad_gate[rows, cols], grad_up[rows, cols] = parts

        @pl.loop(0, depth // TILE)
        def _(c):
            cols = pl.ds(pl.multiple_of(c * TILE, TILE), TILE)
            sums = lax.dot_general(
                grad_gate[rows, :],
                gate_mat[cols, :],
                contract_cols,
                preferred_element_type=jnp.float32,
            ) + lax.dot_general(
                grad_up[rows, :],
                up_mat[cols, :],
                contract_cols,
                preferred_element_type=jnp.float32,
            )
            sums = sums.astype(jnp.bfloat16)
            if g + span < groups:
                slot_grad[rows, cols] = sums
            else:
                for i in range(GROUP):
                    last[i][:, cols] = sums[i * MOST : (i + 1) * MOST]

    def send_back(rows):
        for k in rows:
            if k == 0:
                returned[pl.ds(0, MOST), :] = slot_grad[pl.ds(0, MOST), :]
            else:
                back_copies[k].start()

    for load in loads:
        load.wait()
    near_groups = groups // 2
    pre_stage(0, near_groups)
    pre_stage(near_groups)
    act_stage(0, near_groups)
    act_stage(near_groups)
    back_stage(0, near_groups + 1)
    for g in range(near_groups):
        send_back(members(g))
    held = members(near_groups)[GROUP // 2 :]
    send_back(members(near_groups)[: GROUP // 2])
    pre_stage(groups - 1)
    act_stage(groups - 1)
    send_back(held)
    back_stage(groups - 1)

    for copies in (tok_copies, grad_copies):
        for copy in copies.values():
            copy.wait_send()
    for g in range(groups):
        pre_copies[g].wait_send()
        act_copies[g].wait_send()
    for copy in back_copies.values():
        copy.wait()


def exchange(owners, send_tokens, send_grads, gate_mat, up_mat, down_mat):
    slots, depth = send_tokens.shape
    width = gate_mat.shape[1]
    groups = owners // GROUP
    bf16 = jnp.bfloat16
    wide = jax.ShapeDtypeStruct((slots, depth), bf16)
    back = jax.ShapeDtypeStruct((slots - GROUP * MOST, depth), bf16)
    piece = jax.ShapeDtypeStruct((MOST, depth), bf16)
    thin = jax.ShapeDtypeStruct((slots, width), bf16)
    dma = pltpu.SemaphoreType.DMA
    return pl.pallas_call(
        functools.partial(exchange_kernel, owners),
        out_shape=(wide, wide, thin, thin, thin, back) + (piece,) * GROUP,
        in_specs=[pl.BlockSpec(memory_space=pl.ANY)] * 5,
        out_specs=[pl.BlockSpec(memory_space=pltpu.VMEM)] * (6 + GROUP),
        scratch_shapes=[
            pltpu.VMEM((depth, width), bf16),
            pltpu.VMEM((depth, width), bf16),
            pltpu.VMEM((width, depth), bf16),
            pltpu.VMEM((slots, 2 * width), bf16),
            pltpu.VMEM((slots, width), bf16),
            pltpu.VMEM((slots, 2 * width), bf16),
            pltpu.VMEM((slots, width), bf16),
            pltpu.VMEM((slots - GROUP * MOST, depth), bf16),
            dma((3,)),
            dma((2,)),
        ]
        + [dma((owners,))] * 4
        + [dma((groups,))] * 4
        + [dma((owners - GROUP,))] * 2,
        compiler_params=pltpu.CompilerParams(
            collective_id=0, has_side_effects=True, vmem_limit_bytes=56 * 1024 * 1024
        ),
        cost_estimate=pl.CostEstimate(
            flops=10 * slots * depth * width,
            bytes_accessed=6 * depth * width + 10 * slots * depth + 6 * slots * width,
            transcendentals=slots * width,
        ),
        name="exchange",
    )(send_tokens, send_grads, gate_mat, up_mat, down_mat)


def fused_shards(tokens, out_grad, expert_ids, gate_probs, w_gate, w_up, w_down):
    tok_rows = tokens.shape[0]
    owners = lax.axis_size("expert")
    slots = owners * MOST
    me = lax.axis_index("expert").astype(jnp.int32)
    pick_ids = expert_ids.T.reshape(-1)
    order = jnp.arange(2 * tok_rows, dtype=jnp.int32)
    earlier = (pick_ids[:, None] == pick_ids[None, :]) & (order[:, None] < order[None, :])
    rank_in = jnp.sum(earlier.astype(jnp.int32), axis=0)
    slot_of = ((pick_ids ^ me) * MOST + rank_in).reshape(2, tok_rows)
    slot_ids = jnp.arange(slots, dtype=jnp.int32)[:, None]
    first = slot_ids == slot_of[0][None, :]
    second = slot_ids == slot_of[1][None, :]
    placing = (first | second).astype(jnp.bfloat16)
    slot_prob = jnp.sum(
        jnp.where(first, gate_probs[:, 0][None, :], 0.0)
        + jnp.where(second, gate_probs[:, 1][None, :], 0.0),
        axis=1,
    )
    send_tokens = jnp.dot(placing, tokens, preferred_element_type=jnp.float32).astype(jnp.bfloat16)
    send_grads = (
        slot_prob[:, None] * jnp.dot(placing, out_grad, preferred_element_type=jnp.float32)
    ).astype(jnp.bfloat16)
    got_tokens, got_grads, hidden, grad_gate, grad_up, returned, *last = exchange(
        owners, send_tokens, send_grads, w_gate[0], w_up[0], w_down[0]
    )

    early = slots - GROUP * MOST
    last = [
        lax.ppermute(rows, "expert", [(i, i ^ (owners - GROUP + k)) for i in range(owners)])
        for k, rows in enumerate(last)
    ]

    def outer(left, right):
        return lax.dot_general(left, right, contract_rows, preferred_element_type=jnp.float32)[None]

    token_grad = lax.dot_general(
        placing[:early], returned, contract_rows, preferred_element_type=jnp.float32
    )
    token_grad = token_grad + lax.dot_general(
        placing[early:],
        jnp.concatenate(last, axis=0),
        contract_rows,
        preferred_element_type=jnp.float32,
    )
    token_grad = token_grad.astype(jnp.bfloat16)
    return (
        token_grad,
        outer(got_tokens, grad_gate),
        outer(got_tokens, grad_up),
        outer(hidden, got_grads),
    )


def fits_fused(mesh):
    owners = mesh.shape["expert"]
    return mesh.shape["dp"] == 2 and owners == 4 * GROUP


def solution(mesh):
    in_specs = (
        P("expert", "dp"),
        P("expert", "dp"),
        P("expert", None),
        P("expert", None),
        P("expert", "dp", None),
        P("expert", "dp", None),
        P("expert", None, "dp"),
    )
    out_specs = (
        P("expert", "dp"),
        P("expert", "dp", None),
        P("expert", "dp", None),
        P("expert", None, "dp"),
    )
    body = fused_shards if fits_fused(mesh) else shards
    return jax.shard_map(body, mesh=mesh, in_specs=in_specs, out_specs=out_specs, check_vma=False)
```
